32 devices in a mesh: body: 2 (over y), row: 4 (over x, core), col: 4 (over z).
Axes of the slice: x: 2, y: 2, z: 4, core: 2. Of those that a mesh axis runs over, the one named last changes fastest.
Arguments:
- lam_start: float32 [2, 128, 16384], P('body', None, ('row', 'col')), may hold values from -8 to 8
- load: float32 [2, 128, 16384], P('body', None, ('row', 'col')), may hold values from -24 to 24
- operator: bfloat16 [2, 16384, 4, 4, 1024], P('body', 'row', None, 'col'), as said below
- partner: int32 [2, 16384], P('body', ('row', 'col')), may hold values from 0 to 16383, as said below
- active: int32 [16384], P(('row', 'col')), may hold values 0 or 1
- bounds: int32 [2, 2], P('body'), may hold values from 1 to 20, as said below
Outputs:
- multipliers: float32 [2, 128, 16384], P('body', None, ('row', 'col'))
- residual: float32 [2, 128, 16384], P('body', None, ('row', 'col'))
The draws below stay inside these ranges and needn't reach their ends.
Inputs may be any that keep to these rules, and one draw needn't show every extreme that they name: Each operator F_b is symmetric, with positive diagonal. partner[0] maps every aligned block of 1024 unknowns onto itself, one to one, and partner[1] is its inverse: partner[1, partner[0, i]] = i. bounds[b, 0] is 1 or 2 and bounds[b, 1] is 18 to 20.
All inputs are finite; a program needn't handle non-finite values. No bound on the sum of `active` on one device may be relied on, other than what follows from the above.
Results may differ from the reference program's by a relative error of at most 0.03.
The reference program's roundings to bfloat16 on the way count: a program that leaves them out, or rounds other values in their place, can miss the bound.
Values may be sent and summed in bfloat16 or wider, within the bound.
A program may use at most 128 MiB of HBM per device.

```python
import jax
import jax.numpy as jnp
from jax import lax

M = 16384
R = 128
K = 4
PIECE = 1024
BODIES = 2
N_ROW = 4
N_COL = 4


def draw_operator(key, part):
    keys = jax.random.split(jax.random.fold_in(key, 11), 2)

    def single(subkey):
        first_key, second_key = jax.random.split(subkey, 2)
        noise = jax.random.normal(first_key, (M, M), jnp.float32)
        sym = (noise + noise.T) * (1.4142135 / jnp.sqrt(jnp.float32(M)))
        diag_vals = jax.random.uniform(second_key, (M,), jnp.float32, 6.0, 14.0)
        idx = jnp.arange(M)
        sym = sym.at[idx, idx].add(diag_vals)
        return sym.astype(jnp.bfloat16)
    return lax.map(single, keys).reshape(2, M, N_ROW, N_COL, PIECE)


def draw_partner(key, part):
    blocks = M // PIECE
    keys = jax.random.split(jax.random.fold_in(key, 23), blocks)
    perms = jax.vmap(lambda subkey: jax.random.permutation(subkey, PIECE))(keys).astype(jnp.int32)
    offsets = (jnp.arange(blocks, dtype=jnp.int32) * PIECE)[:, None]
    forward = (perms + offsets).reshape(M)
    inverse = jnp.argsort(forward, stable=True).astype(jnp.int32)
    return jnp.stack([forward, inverse])


def draw_bounds(key, part):
    first_key, second_key = jax.random.split(jax.random.fold_in(key, 37))
    lower = jax.random.randint(first_key, (2,), 1, 3, jnp.int32)
    upper = jax.random.randint(second_key, (2,), 18, 21, jnp.int32)
    return jnp.stack([lower, upper], axis=1)


def touch_ends(drawn, key, smallest, high):
    extent = drawn.shape
    place = [jax.random.randint(jax.random.fold_in(key, axis), (), 0, extent[axis]) for axis in range(len(extent))]
    drawn = drawn.at[tuple(place)].set(smallest)
    longest = extent.index(max(extent))
    place[longest] = (place[longest] + 1) % extent[longest]
    return drawn.at[tuple(place)].set(high)


def block_levels(own_key, dims, shards, low, high):
    factor_of, own = 1.0, jax.random.fold_in(own_key, 6)
    for axis_at, shards_of in shards:
        steps = jnp.exp(jax.random.uniform(jax.random.fold_in(own, axis_at), (shards_of,), jnp.float32, low / len(shards), high / len(shards)))
        factor_of = factor_of * jnp.repeat(steps, dims[axis_at] // shards_of).reshape([-1 if axis == axis_at else 1 for axis in range(len(dims))])
    return factor_of


def normal_values(stream_key, shape, width, limit, cuts=(), held_as=jnp.bfloat16):
    values = jax.random.normal(stream_key, shape, jnp.float32) * width
    if len(cuts) > 0:
        values = block_levels(stream_key, shape, cuts, -0.22, 0.18) * values
    return jnp.clip(values, min=-limit, max=limit).astype(held_as)


def setup_inputs(seed: int = 0) -> dict:
    seeds = jax.random.split(jax.random.key(seed), 7)
    return {
        "lam_start": normal_values(seeds[0], (BODIES, R, M), 3.0, 8.0, ((0, 2), (2, 16)), jnp.float32),
        "load": normal_values(seeds[1], (BODIES, R, M), 4.0, 24.0, ((0, 2), (2, 16)), jnp.float32),
        "operator": draw_operator(jax.random.fold_in(seeds[6], 71), 0),
        "partner": draw_partner(jax.random.fold_in(seeds[6], 71), 0),
        "active": touch_ends((jax.random.randint(seeds[4], (M,), 0, 2) < 1).astype(jnp.int32), jax.random.fold_in(seeds[4], 1), 0, 1),
        "bounds": draw_bounds(jax.random.fold_in(seeds[6], 71), 0),
    }


def apply_all(field, dense):
    rounded = field.astype(jnp.bfloat16)
    outs = []
    for which in range(2):
        outs.append(lax.dot_general(rounded[which], dense[which], (((1,), (1,)), ((), ())), preferred_element_type=jnp.float32))
    return jnp.stack(outs)


def clamp_all(lam, partner, active):
    mate = jnp.stack([jnp.take(lam[1], partner[0], axis=1), jnp.take(lam[0], partner[1], axis=1)])
    flags = jnp.stack([active, jnp.take(active, partner[1])]) > 0
    sign = jnp.array([1.0, -1.0], jnp.float32)[:, None, None]
    middle = 0.5 * (lam + mate)
    normal = 0.5 * sign * (lam - mate)
    normal = jnp.where(flags[:, None, :], jnp.maximum(normal, 0.0), normal)
    return middle + sign * normal


def cheb_pass(start, load, dense, bounds):
    lower = bounds[:, 0].astype(jnp.float32)[:, None, None]
    upper = bounds[:, 1].astype(jnp.float32)[:, None, None]
    theta = 0.5 * (upper + lower)
    delta = 0.5 * (upper - lower)
    sigma = theta / delta
    answer = start
    resid = load - apply_all(answer, dense)
    direction = resid / theta
    rho = delta / theta
    for step in range(K):
        answer = answer + direction
        resid = resid - apply_all(direction, dense)
        if step + 1 < K:
            rho_new = 1.0 / (2.0 * sigma - rho)
            direction = rho_new * rho * direction + (2.0 * rho_new / delta) * resid
            rho = rho_new
    return answer, resid


def reference(lam_start, load, operator, partner, active, bounds):
    dense = operator.reshape(2, M, M)
    first = clamp_all(lam_start, partner, active)
    second, unused = cheb_pass(first, load, dense, bounds)
    third = clamp_all(second, partner, active)
    return cheb_pass(third, load, dense, bounds)
```

```python
import functools

import jax
import jax.numpy as jnp
from jax import lax
from jax.experimental import pallas as pl
from jax.experimental.pallas import tpu as pltpu
from jax.sharding import PartitionSpec as P

K = 4
GROUPS = 2
MESH = pl.DeviceIdType.MESH


def kernel(
    n_row, n_col, coef_ref, lam_ref, load_ref, tile_hbm, partner_ref, active_ref, x_ref, r_ref,
    tile, gathered, partial, core_in, far_out, far_in, peer0, peer1, select, flags, direction,
    tile_sem, own_send, pass_send, col_recv, core_send, core_recv, far_send, far_recv, peer_send, peer_recv,
):
    rows, width = lam_ref.shape
    part = rows // GROUPS
    n_far = n_row // 2
    applies = 2 * K + 1
    hub = n_col == 4
    body = lax.axis_index("body")
    row = lax.axis_index("row")
    col = lax.axis_index("col")
    core = row % 2
    far = row // 2
    core_peer = row + 1 - 2 * core
    if hub:
        col_mate = col + 1 - 2 * (col % 2)
        inner_over = 2 - col // 2
        end_over = 3 - 3 * (col // 2)
        order = [col, col_mate, inner_over, end_over]
        targets = [col_mate, inner_over]
    else:
        order = [(col + shift) % n_col for shift in range(n_col)]
        targets = [(col + shift) % n_col for shift in range(1, n_col)]
    inner = ((col + 1) // 2) % 2 == 1

    tile_copy = pltpu.make_async_copy(tile_hbm, tile, tile_sem)
    tile_copy.start()

    barrier = pltpu.get_barrier_semaphore()
    for shift in range(1, n_col):
        pl.semaphore_signal(barrier, inc=1, device_id={"col": (col + shift) % n_col}, device_id_type=MESH)
    for shift in range(1, n_row):
        pl.semaphore_signal(barrier, inc=1, device_id={"row": (row + shift) % n_row}, device_id_type=MESH)
    pl.semaphore_signal(barrier, inc=1, device_id={"body": 1 - body}, device_id_type=MESH)
    pl.semaphore_wait(barrier, n_col + n_row - 1)

    def peer_copy(source, target, slot):
        return pltpu.make_async_remote_copy(
            src_ref=source, dst_ref=target, send_sem=peer_send.at[slot], recv_sem=peer_recv.at[slot],
            device_id={"body": 1 - body}, device_id_type=MESH,
        )

    def col_copy(parity, group, source, target, send_sem):
        block = gathered.at[parity, group, source]
        return pltpu.make_async_remote_copy(
            src_ref=block, dst_ref=block, send_sem=send_sem, recv_sem=col_recv.at[parity, group, source],
            device_id={"col": target}, device_id_type=MESH,
        )

    def own_copies(parity, group):
        return [
            col_copy(parity, group, col, target, own_send.at[group, at]) for at, target in enumerate(targets)
        ]

    def core_copy(parity, group):
        return pltpu.make_async_remote_copy(
            src_ref=partial.at[group, 1 - core], dst_ref=core_in.at[parity, group],
            send_sem=core_send.at[group], recv_sem=core_recv.at[parity, group],
            device_id={"row": core_peer}, device_id_type=MESH,
        )

    def far_copy(parity, group, shift):
        return pltpu.make_async_remote_copy(
            src_ref=far_out.at[group, shift - 1], dst_ref=far_in.at[parity, group, shift - 1],
            send_sem=far_send.at[group, shift - 1], recv_sem=far_recv.at[parity, group, shift - 1],
            device_id={"row": ((far + shift) % n_far) * 2 + core}, device_id_type=MESH,
        )

    first = peer_copy(lam_ref, peer0, 0)
    first.start()

    which = jnp.broadcast_to(partner_ref[...] % width, (width, width))
    select[...] = jnp.where(
        lax.broadcasted_iota(jnp.int32, (width, width), 0) == which, 1.0, 0.0
    ).astype(jnp.bfloat16)
    active = active_ref[...].astype(jnp.float32)
    spread = jnp.broadcast_to(active, (16, width)).astype(jnp.bfloat16)
    moved = jnp.dot(spread, select[...], preferred_element_type=jnp.float32)[:1]
    flags[...] = jnp.where(body == 0, active, moved)
    sign = (1 - 2 * body).astype(jnp.float32)
    r_ref[...] = load_ref[...]
    direction[...] = jnp.zeros_like(direction)

    def clamp(lam, peer):
        high = peer.astype(jnp.bfloat16)
        rest = peer - high.astype(jnp.float32)
        middle_piece = rest.astype(jnp.bfloat16)
        low = (rest - middle_piece.astype(jnp.float32)).astype(jnp.bfloat16)
        mate = jnp.dot(high, select[...], preferred_element_type=jnp.float32)
        mate = mate + jnp.dot(middle_piece, select[...], preferred_element_type=jnp.float32)
        mate = mate + jnp.dot(low, select[...], preferred_element_type=jnp.float32)
        middle = 0.5 * (lam + mate)
        normal = 0.5 * sign * (lam - mate)
        normal = jnp.where(flags[...] > 0.5, jnp.maximum(normal, 0.0), normal)
        return middle + sign * normal

    def multiply(parity, group, source, start):
        def one(q, carry):
            columns = pl.ds(pl.multiple_of(q * width, width), width)
            depth = pl.ds(pl.multiple_of(source * width, width), width)
            product = jnp.dot(gathered[parity, group, source], tile[depth, columns], preferred_element_type=jnp.float32)
            if start:
                partial[group, q % 2, q // 2] = product
            else:
                partial[group, q % 2, q // 2] += product
            return carry

        lax.fori_loop(0, n_row, one, 0)

    def begin(parity, group, value):
        gathered[parity, group, col] = value.astype(jnp.bfloat16)
        for copy in own_copies(parity, group):
            copy.start()

    first.wait()
    for group in range(GROUPS):
        band = pl.ds(group * part, part)
        start = clamp(lam_ref[band, :], peer0[band, :])
        x_ref[band, :] = start
        begin(0, group, start)
    tile_copy.wait()

    def half_step(h, carry):
        group = h % GROUPS
        time = h // GROUPS
        parity = time % 2
        late = (h + GROUPS - 1) % GROUPS
        late_time = (h + GROUPS - 1) // GROUPS - 1
        late_parity = (late_time + 2) % 2
        live = h < applies * GROUPS

        @pl.when(live)
        def _():
            multiply(parity, group, order[0], True)

        @pl.when(h >= 1)
        def _():
            core_copy(late_parity, late).wait()
            for shift in range(1, n_far):
                other = (far + shift) % n_far
                far_out[late, shift - 1] = partial[late, core, other] + core_in[late_parity, late, other]
                far_copy(late_parity, late, shift).start()

        def take(at):
            source = order[at]
            col_copy(parity, group, source, source, own_send.at[group, 0]).wait_recv()
            if hub and at >= 2:
                @pl.when(inner)
                def _():
                    col_copy(parity, group, source, col_mate, pass_send.at[group, at - 2]).start()
            multiply(parity, group, source, False)

        @pl.when(live)
        def _():
            for at in range(1, n_col - 1):
                take(at)

        @pl.when(h >= 1)
        def _():
            total = partial[late, core, far] + core_in[late_parity, late, far]
            for shift in range(1, n_far):
                far_copy(late_parity, late, shift).wait()
                total = total + far_in[late_parity, late, shift - 1]
            for copy in own_copies(late_parity, late):
                copy.wait_send()
            if hub:
                @pl.when(inner)
                def _():
                    for at in range(2):
                        col_copy(late_parity, late, order[at + 2], col_mate, pass_send.at[late, at]).wait_send()
            band = pl.ds(pl.multiple_of(late * part, part), part)
            resid = r_ref[band, :] - total
            r_ref[band, :] = resid

            @pl.when(late_time != 2 * K)
            def _():
                step = late_time % K
                move = coef_ref[step] * direction[band, :] + coef_ref[K + step] * resid
                direction[band, :] = move
                answer = x_ref[band, :] + move
                x_ref[band, :] = answer

                @pl.when(late_time != K - 1)
                def _():
                    begin(1 - late_parity, late, move)

                @pl.when(late_time == K - 1)
                def _():
                    exchange = peer_copy(x_ref.at[band, :], peer1.at[band, :], 1 + late)
                    exchange.start()
                    exchange.wait()
                    again = clamp(x_ref[band, :], peer1[band, :])
                    x_ref[band, :] = again
                    r_ref[band, :] = load_ref[band, :]
                    begin(1 - late_parity, late, again)

        @pl.when(live)
        def _():
            take(n_col - 1)
            core_copy(parity, group).start()

        return carry

    lax.fori_loop(0, applies * GROUPS + 1, half_step, 0)


def coefficients(bounds):
    lower = bounds[0, 0].astype(jnp.float32)
    upper = bounds[0, 1].astype(jnp.float32)
    theta = 0.5 * (upper + lower)
    delta = 0.5 * (upper - lower)
    sigma = theta / delta
    rho = delta / theta
    keep, add = [jnp.zeros_like(theta)], [1.0 / theta]
    for _ in range(K - 1):
        rho_new = 1.0 / (2.0 * sigma - rho)
        keep.append(rho_new * rho)
        add.append(2.0 * rho_new / delta)
        rho = rho_new
    return jnp.stack(keep + add)


def per_device(n_row, n_col, lam_start, load, operator, partner, active, bounds):
    rows, width = lam_start.shape[1:]
    tile = operator.reshape(operator.shape[1], operator.shape[2] * operator.shape[4])
    part = rows // GROUPS
    n_far = n_row // 2
    f32, bf16 = jnp.float32, jnp.bfloat16
    vmem = pl.BlockSpec(memory_space=pltpu.VMEM)
    dma = pltpu.SemaphoreType.DMA
    flops = 2 * (2 * K + 1) * rows * tile.shape[0] * tile.shape[1]
    answer, resid = pl.pallas_call(
        functools.partial(kernel, n_row, n_col),
        out_shape=[jax.ShapeDtypeStruct((rows, width), f32)] * 2,
        in_specs=[
            pl.BlockSpec(memory_space=pltpu.SMEM), vmem, vmem, pl.BlockSpec(memory_space=pl.ANY), vmem, vmem,
        ],
        out_specs=[vmem, vmem],
        scratch_shapes=[
            pltpu.VMEM(tile.shape, bf16),
            pltpu.VMEM((2, GROUPS, n_col, part, width), bf16),
            pltpu.VMEM((GROUPS, 2, n_far, part, width), f32),
            pltpu.VMEM((2, GROUPS, n_far, part, width), f32),
            pltpu.VMEM((GROUPS, n_far - 1, part, width), f32),
            pltpu.VMEM((2, GROUPS, n_far - 1, part, width), f32),
            pltpu.VMEM((rows, width), f32),
            pltpu.VMEM((rows, width), f32),
            pltpu.VMEM((width, width), bf16),
            pltpu.VMEM((1, width), f32),
            pltpu.VMEM((rows, width), f32),
            dma,
            dma((GROUPS, n_col - 1)),
            dma((GROUPS, 2)),
            dma((2, GROUPS, n_col)),
            dma((GROUPS,)),
            dma((2, GROUPS)),
            dma((GROUPS, n_far - 1)),
            dma((2, GROUPS, n_far - 1)),
            dma((1 + GROUPS,)),
            dma((1 + GROUPS,)),
        ],
        compiler_params=pltpu.CompilerParams(
            collective_id=0, has_side_effects=True, vmem_limit_bytes=58 * 1024 * 1024
        ),
        cost_estimate=pl.CostEstimate(flops=flops, bytes_accessed=2 * tile.size, transcendentals=0),
    )(coefficients(bounds), lam_start[0], load[0], tile, partner, active[None])
    return (answer[None], resid[None])


def solution(mesh):
    return jax.shard_map(
        functools.partial(per_device, mesh.shape["row"], mesh.shape["col"]),
        mesh=mesh,
        in_specs=(
            P("body", None, ("row", "col")),
            P("body", None, ("row", "col")),
            P("body", "row", None, "col", None),
            P("body", ("row", "col")),
            P(("row", "col")),
            P("body", None),
        ),
        out_specs=(P("body", None, ("row", "col")), P("body", None, ("row", "col"))),
        check_vma=False,
    )
```

```python
import functools

import jax
import jax.numpy as jnp
from jax import lax
from jax.experimental import pallas as pl
from jax.experimental.pallas import tpu as pltpu
from jax.sharding import PartitionSpec as P

K = 4
GROUPS = 2
MESH = pl.DeviceIdType.MESH


def kernel(
    n_row, n_col, coef_ref, lam_ref, load_ref, tile_hbm, partner_ref, active_ref, x_ref, r_ref,
    tile, gathered, partial, core_in, far_out, far_in, peer0, peer1, select, flags, direction,
    tile_sem, own_send, pass_send, col_recv, core_send, core_recv, far_send, far_recv, peer_send, peer_recv,
):
    rows, width = lam_ref.shape
    part = rows // GROUPS
    n_far = n_row // 2
    applies = 2 * K + 1
    hub = n_col == 4
    body = lax.axis_index("body")
    row = lax.axis_index("row")
    col = lax.axis_index("col")
    core = row % 2
    far = row // 2
    core_peer = row + 1 - 2 * core
    if hub:
        col_mate = col + 1 - 2 * (col % 2)
        inner_over = 2 - col // 2
        end_over = 3 - 3 * (col // 2)
        order = [col, col_mate, inner_over, end_over]
        targets = [col_mate, inner_over]
    else:
        order = [(col + shift) % n_col for shift in range(n_col)]
        targets = [(col + shift) % n_col for shift in range(1, n_col)]
    inner = ((col + 1) // 2) % 2 == 1

    tile_copy = pltpu.make_async_copy(tile_hbm, tile, tile_sem)
    tile_copy.start()

    barrier = pltpu.get_barrier_semaphore()
    for shift in range(1, n_col):
        pl.semaphore_signal(barrier, inc=1, device_id={"col": (col + shift) % n_col}, device_id_type=MESH)
    for shift in range(1, n_row):
        pl.semaphore_signal(barrier, inc=1, device_id={"row": (row + shift) % n_row}, device_id_type=MESH)
    pl.semaphore_signal(barrier, inc=1, device_id={"body": 1 - body}, device_id_type=MESH)
    pl.semaphore_wait(barrier, n_col + n_row - 1)

    def peer_copy(source, target, slot):
        return pltpu.make_async_remote_copy(
            src_ref=source, dst_ref=target, send_sem=peer_send.at[slot], recv_sem=peer_recv.at[slot],
            device_id={"body": 1 - body}, device_id_type=MESH,
        )

    def col_copy(parity, group, source, target, send_sem):
        block = gathered.at[parity, group, source]
        return pltpu.make_async_remote_copy(
            src_ref=block, dst_ref=block, send_sem=send_sem, recv_sem=col_recv.at[parity, group, source],
            device_id={"col": target}, device_id_type=MESH,
        )

    def own_copies(parity, group):
        return [
            col_copy(parity, group, col, target, own_send.at[group, at]) for at, target in enumerate(targets)
        ]

    def core_copy(parity, group):
        return pltpu.make_async_remote_copy(
            src_ref=partial.at[group, 1 - core], dst_ref=core_in.at[parity, group],
            send_sem=core_send.at[group], recv_sem=core_recv.at[parity, group],
            device_id={"row": core_peer}, device_id_type=MESH,
        )

    def far_copy(parity, group, shift):
        return pltpu.make_async_remote_copy(
            src_ref=far_out.at[group, shift - 1], dst_ref=far_in.at[parity, group, shift - 1],
            send_sem=far_send.at[group, shift - 1], recv_sem=far_recv.at[parity, group, shift - 1],
            device_id={"row": ((far + shift) % n_far) * 2 + core}, device_id_type=MESH,
        )

    bands = [pl.ds(group * part, part) for group in range(GROUPS)]
    first = [peer_copy(lam_ref.at[band, :], peer0.at[band, :], GROUPS + at) for at, band in enumerate(bands)]
    for copy in first:
        copy.start()

    which = jnp.broadcast_to(partner_ref[...] % width, (width, width))
    select[...] = jnp.where(
        lax.broadcasted_iota(jnp.int32, (width, width), 0) == which, 1.0, 0.0
    ).astype(jnp.bfloat16)
    active = active_ref[...].astype(jnp.float32)
    spread = jnp.broadcast_to(active, (16, width)).astype(jnp.bfloat16)
    moved = jnp.dot(spread, select[...], preferred_element_type=jnp.float32)[:1]
    flags[...] = jnp.where(body == 0, active, moved)
    sign = (1 - 2 * body).astype(jnp.float32)
    r_ref[...] = load_ref[...]
    direction[...] = jnp.zeros_like(direction)

    def clamp(lam, peer):
        high = peer.astype(jnp.bfloat16)
        rest = peer - high.astype(jnp.float32)
        middle_piece = rest.astype(jnp.bfloat16)
        low = (rest - middle_piece.astype(jnp.float32)).astype(jnp.bfloat16)
        mate = jnp.dot(high, select[...], preferred_element_type=jnp.float32)
        mate = mate + jnp.dot(middle_piece, select[...], preferred_element_type=jnp.float32)
        mate = mate + jnp.dot(low, select[...], preferred_element_type=jnp.float32)
        middle = 0.5 * (lam + mate)
        normal = 0.5 * sign * (lam - mate)
        normal = jnp.where(flags[...] > 0.5, jnp.maximum(normal, 0.0), normal)
        return middle + sign * normal

    def multiply(parity, group, source, start, low=0, high=n_row):
        def one(at, carry):
            to_core = (core + 1 + at // n_far) % 2
            to_far = (far + 1 + at) % n_far
            columns = pl.ds(pl.multiple_of((to_far * 2 + to_core) * width, width), width)
            depth = pl.ds(pl.multiple_of(source * width, width), width)
            product = jnp.dot(gathered[parity, group, source], tile[depth, columns], preferred_element_type=jnp.float32)
            if start:
                partial[group, to_core, to_far] = product
            else:
                partial[group, to_core, to_far] += product
            return carry

        lax.fori_loop(low, high, one, 0)

    def begin(parity, group, value):
        gathered[parity, group, col] = value.astype(jnp.bfloat16)
        for copy in own_copies(parity, group):
            copy.start()

    for group, band in enumerate(bands):
        first[group].wait()
        start = clamp(lam_ref[band, :], peer0[band, :])
        x_ref[band, :] = start
        begin(0, group, start)
    tile_copy.wait()

    def half_step(h, carry):
        group = h % GROUPS
        time = h // GROUPS
        parity = time % 2
        late = (h + GROUPS - 1) % GROUPS
        late_time = (h + GROUPS - 1) // GROUPS - 1
        late_parity = (late_time + 2) % 2
        live = h < applies * GROUPS

        @pl.when(h >= 1)
        def _():
            core_copy(late_parity, late).wait()
            for shift in range(1, n_far):
                other = (far + shift) % n_far
                far_out[late, shift - 1] = partial[late, core, other] + core_in[late_parity, late, other]
                far_copy(late_parity, late, shift).start()

        @pl.when(live & (time == K))
        def _():
            band = pl.ds(pl.multiple_of(group * part, part), part)
            peer_copy(x_ref.at[band, :], peer1.at[band, :], group).wait()
            again = clamp(x_ref[band, :], peer1[band, :])
            x_ref[band, :] = again
            r_ref[band, :] = load_ref[band, :]
            begin(parity, group, again)

        def arrive(at):
            col_copy(parity, group, order[at], order[at], own_send.at[group, 0]).wait_recv()

        def pass_on(at):
            @pl.when(inner)
            def _():
                arrive(at)
                col_copy(parity, group, order[at], col_mate, pass_send.at[group, at - 2]).start()

        def take(at):
            if hub and at >= 2:
                @pl.when(jnp.logical_not(inner))
                def _():
                    arrive(at)
            else:
                arrive(at)

        @pl.when(live)
        def _():
            if hub:
                pass_on(2)
            multiply(parity, group, order[0], True)
            if hub:
                pass_on(3)
            for at in range(1, n_col - 1):
                take(at)
                multiply(parity, group, order[at], False)

        @pl.when(h >= 1)
        def _():
            total = partial[late, core, far] + core_in[late_parity, late, far]
            for shift in range(1, n_far):
                far_copy(late_parity, late, shift).wait()
                total = total + far_in[late_parity, late, shift - 1]
            for copy in own_copies(late_parity, late):
                copy.wait_send()
            if hub:
                @pl.when(inner)
                def _():
                    for at in range(2):
                        col_copy(late_parity, late, order[at + 2], col_mate, pass_send.at[late, at]).wait_send()
            band = pl.ds(pl.multiple_of(late * part, part), part)
            resid = r_ref[band, :] - total
            r_ref[band, :] = resid

            @pl.when(late_time != 2 * K)
            def _():
                step = late_time % K
                move = coef_ref[step] * direction[band, :] + coef_ref[K + step] * resid
                direction[band, :] = move
                answer = x_ref[band, :] + move
                x_ref[band, :] = answer

                @pl.when(late_time != K - 1)
                def _():
                    begin(1 - late_parity, late, move)

                @pl.when(late_time == K - 1)
                def _():
                    peer_copy(x_ref.at[band, :], peer1.at[band, :], late).start()

        @pl.when(live)
        def _():
            take(n_col - 1)
            multiply(parity, group, order[n_col - 1], False, 0, n_far)
            core_copy(parity, group).start()
            multiply(parity, group, order[n_col - 1], False, n_far, n_row)

        return carry

    lax.fori_loop(0, applies * GROUPS + 1, half_step, 0)


def coefficients(bounds):
    lower = bounds[0, 0].astype(jnp.float32)
    upper = bounds[0, 1].astype(jnp.float32)
    theta = 0.5 * (upper + lower)
    delta = 0.5 * (upper - lower)
    sigma = theta / delta
    rho = delta / theta
    keep, add = [jnp.zeros_like(theta)], [1.0 / theta]
    for _ in range(K - 1):
        rho_new = 1.0 / (2.0 * sigma - rho)
        keep.append(rho_new * rho)
        add.append(2.0 * rho_new / delta)
        rho = rho_new
    return jnp.stack(keep + add)


def per_device(n_row, n_col, lam_start, load, operator, partner, active, bounds):
    rows, width = lam_start.shape[1:]
    tile = operator.reshape(operator.shape[1], operator.shape[2] * operator.shape[4])
    part = rows // GROUPS
    n_far = n_row // 2
    f32, bf16 = jnp.float32, jnp.bfloat16
    vmem = pl.BlockSpec(memory_space=pltpu.VMEM)
    dma = pltpu.SemaphoreType.DMA
    flops = 2 * (2 * K + 1) * rows * tile.shape[0] * tile.shape[1]
    answer, resid = pl.pallas_call(
        functools.partial(kernel, n_row, n_col),
        out_shape=[jax.ShapeDtypeStruct((rows, width), f32)] * 2,
        in_specs=[
            pl.BlockSpec(memory_space=pltpu.SMEM), vmem, vmem, pl.BlockSpec(memory_space=pl.ANY), vmem, vmem,
        ],
        out_specs=[vmem, vmem],
        scratch_shapes=[
            pltpu.VMEM(tile.shape, bf16),
            pltpu.VMEM((2, GROUPS, n_col, part, width), bf16),
            pltpu.VMEM((GROUPS, 2, n_far, part, width), f32),
            pltpu.VMEM((2, GROUPS, n_far, part, width), f32),
            pltpu.VMEM((GROUPS, n_far - 1, part, width), f32),
            pltpu.VMEM((2, GROUPS, n_far - 1, part, width), f32),
            pltpu.VMEM((rows, width), f32),
            pltpu.VMEM((rows, width), f32),
            pltpu.VMEM((width, width), bf16),
            pltpu.VMEM((1, width), f32),
            pltpu.VMEM((rows, width), f32),
            dma,
            dma((GROUPS, n_col - 1)),
            dma((GROUPS, 2)),
            dma((2, GROUPS, n_col)),
            dma((GROUPS,)),
            dma((2, GROUPS)),
            dma((GROUPS, n_far - 1)),
            dma((2, GROUPS, n_far - 1)),
            dma((2 * GROUPS,)),
            dma((2 * GROUPS,)),
        ],
        compiler_params=pltpu.CompilerParams(
            collective_id=0, has_side_effects=True, vmem_limit_bytes=58 * 1024 * 1024
        ),
        cost_estimate=pl.CostEstimate(flops=flops, bytes_accessed=2 * tile.size, transcendentals=0),
    )(coefficients(bounds), lam_start[0], load[0], tile, partner, active[None])
    return (answer[None], resid[None])


def solution(mesh):
    return jax.shard_map(
        functools.partial(per_device, mesh.shape["row"], mesh.shape["col"]),
        mesh=mesh,
        in_specs=(
            P("body", None, ("row", "col")),
            P("body", None, ("row", "col")),
            P("body", "row", None, "col", None),
            P("body", ("row", "col")),
            P(("row", "col")),
            P("body", None),
        ),
        out_specs=(P("body", None, ("row", "col")), P("body", None, ("row", "col"))),
        check_vma=False,
    )
```

```python
import functools

import jax
import jax.numpy as jnp
from jax import lax
from jax.experimental import pallas as pl
from jax.experimental.pallas import tpu as pltpu
from jax.sharding import PartitionSpec as P

K = 4
GROUPS = 2
MESH = pl.DeviceIdType.MESH


def kernel(
    n_row, n_col, coef_ref, lam_ref, load_ref, tile_hbm, partner_ref, active_ref, x_ref, r_ref,
    tile, raw, wide, gathered, partial, core_in, far_out, far_in, peer0, peer1, select, flags, direction,
    tile_sem, own_send, pass_send, col_recv, core_send, core_recv, far_send, far_recv, peer_send, peer_recv,
):
    rows, width = lam_ref.shape
    part = rows // GROUPS
    n_far = n_row // 2
    applies = 2 * K + 1
    hub = n_col == 4
    body = lax.axis_index("body")
    row = lax.axis_index("row")
    col = lax.axis_index("col")
    core = row % 2
    far = row // 2
    core_peer = row + 1 - 2 * core
    if hub:
        col_mate = col + 1 - 2 * (col % 2)
        inner_over = 2 - col // 2
        end_over = 3 - 3 * (col // 2)
        order = [col, col_mate, inner_over, end_over]
        targets = [col_mate, inner_over]
    else:
        order = [(col + shift) % n_col for shift in range(n_col)]
        targets = [(col + shift) % n_col for shift in range(1, n_col)]
    inner = ((col + 1) // 2) % 2 == 1

    chunk = raw.shape[1]
    chunks = tile_hbm.shape[0] // chunk

    def raw_copy(at):
        return pltpu.make_async_copy(
            tile_hbm.at[pl.ds(pl.multiple_of(at * chunk, chunk), chunk)], raw.at[at % 2], tile_sem.at[at % 2]
        )

    raw_copy(0).start()

    barrier = pltpu.get_barrier_semaphore()
    for shift in range(1, n_col):
        pl.semaphore_signal(barrier, inc=1, device_id={"col": (col + shift) % n_col}, device_id_type=MESH)
    for shift in range(1, n_row):
        pl.semaphore_signal(barrier, inc=1, device_id={"row": (row + shift) % n_row}, device_id_type=MESH)
    pl.semaphore_signal(barrier, inc=1, device_id={"body": 1 - body}, device_id_type=MESH)
    pl.semaphore_wait(barrier, n_col + n_row - 1)

    def peer_copy(source, target, slot):
        return pltpu.make_async_remote_copy(
            src_ref=source, dst_ref=target, send_sem=peer_send.at[slot], recv_sem=peer_recv.at[slot],
            device_id={"body": 1 - body}, device_id_type=MESH,
        )

    def col_copy(parity, group, source, target, send_sem):
        block = gathered.at[parity, group, source]
        return pltpu.make_async_remote_copy(
            src_ref=block, dst_ref=block, send_sem=send_sem, recv_sem=col_recv.at[parity, group, source],
            device_id={"col": target}, device_id_type=MESH,
        )

    def own_copies(parity, group):
        return [
            col_copy(parity, group, col, target, own_send.at[group, at]) for at, target in enumerate(targets)
        ]

    def core_copy(parity, group):
        return pltpu.make_async_remote_copy(
            src_ref=partial.at[group, 1 - core], dst_ref=core_in.at[parity, group],
            send_sem=core_send.at[group], recv_sem=core_recv.at[parity, group],
            device_id={"row": core_peer}, device_id_type=MESH,
        )

    def far_copy(parity, group, shift):
        return pltpu.make_async_remote_copy(
            src_ref=far_out.at[group, shift - 1], dst_ref=far_in.at[parity, group, shift - 1],
            send_sem=far_send.at[group, shift - 1], recv_sem=far_recv.at[parity, group, shift - 1],
            device_id={"row": ((far + shift) % n_far) * 2 + core}, device_id_type=MESH,
        )

    bands = [pl.ds(group * part, part) for group in range(GROUPS)]
    first = [peer_copy(lam_ref.at[band, :], peer0.at[band, :], GROUPS + at) for at, band in enumerate(bands)]
    for copy in first:
        copy.start()

    which = jnp.broadcast_to(partner_ref[...] % width, (width, width))
    select[...] = jnp.where(
        lax.broadcasted_iota(jnp.int32, (width, width), 0) == which, 1.0, 0.0
    ).astype(jnp.bfloat16)
    active = active_ref[...].astype(jnp.float32)
    spread = jnp.broadcast_to(active, (16, width)).astype(jnp.bfloat16)
    moved = jnp.dot(spread, select[...], preferred_element_type=jnp.float32)[:1]
    flags[...] = jnp.where(body == 0, active, moved)
    sign = (1 - 2 * body).astype(jnp.float32)
    r_ref[...] = load_ref[...]
    direction[...] = jnp.zeros_like(direction)

    def clamp(lam, peer):
        high = peer.astype(jnp.bfloat16)
        rest = peer - high.astype(jnp.float32)
        middle_piece = rest.astype(jnp.bfloat16)
        low = (rest - middle_piece.astype(jnp.float32)).astype(jnp.bfloat16)
        mate = jnp.dot(high, select[...], preferred_element_type=jnp.float32)
        mate = mate + jnp.dot(middle_piece, select[...], preferred_element_type=jnp.float32)
        mate = mate + jnp.dot(low, select[...], preferred_element_type=jnp.float32)
        middle = 0.5 * (lam + mate)
        normal = 0.5 * sign * (lam - mate)
        normal = jnp.where(flags[...] > 0.5, jnp.maximum(normal, 0.0), normal)
        return middle + sign * normal

    def multiply(parity, group, source, start, low=0, high=n_row):
        def one(at, carry):
            to_core = (core + 1 + at // n_far) % 2
            to_far = (far + 1 + at) % n_far
            columns = pl.ds(pl.multiple_of((to_far * 2 + to_core) * width, width), width)
            depth = pl.ds(pl.multiple_of(source * width, width), width)
            product = jnp.dot(gathered[parity, group, source], tile[depth, columns], preferred_element_type=jnp.float32)
            if start:
                partial[group, to_core, to_far] = product
            else:
                partial[group, to_core, to_far] += product
            return carry

        lax.fori_loop(low, high, one, 0)

    def begin(parity, group, value):
        gathered[parity, group, col] = value.astype(jnp.bfloat16)
        for copy in own_copies(parity, group):
            copy.start()

    def sort_chunk(at, carry):
        @pl.when(at + 1 < chunks)
        def _():
            raw_copy(at + 1).start()

        raw_copy(at).wait()
        depth = pl.ds(pl.multiple_of(at * chunk, chunk), chunk)
        for lane in range(width // 128):
            slot = lane % 2
            wide[slot] = raw[at % 2, :, :, lane * 128:(lane + 1) * 128].astype(jnp.float32)
            flat = wide.at[slot].reshape(chunk * n_row, 128)
            for q in range(n_row):
                tile[depth, q * width + lane * 128:q * width + (lane + 1) * 128] = flat[
                    pl.ds(q, chunk, stride=n_row), :
                ].astype(jnp.bfloat16)
        return carry

    lax.fori_loop(0, chunks, sort_chunk, 0)
    for group, band in enumerate(bands):
        first[group].wait()
        start = clamp(lam_ref[band, :], peer0[band, :])
        x_ref[band, :] = start
        begin(0, group, start)

    def half_step(h, carry):
        group = h % GROUPS
        time = h // GROUPS
        parity = time % 2
        late = (h + GROUPS - 1) % GROUPS
        late_time = (h + GROUPS - 1) // GROUPS - 1
        late_parity = (late_time + 2) % 2
        live = h < applies * GROUPS

        @pl.when(h >= 1)
        def _():
            core_copy(late_parity, late).wait()
            for shift in range(1, n_far):
                other = (far + shift) % n_far
                far_out[late, shift - 1] = partial[late, core, other] + core_in[late_parity, late, other]
                far_copy(late_parity, late, shift).start()

        @pl.when(live & (time == K))
        def _():
            band = pl.ds(pl.multiple_of(group * part, part), part)
            peer_copy(x_ref.at[band, :], peer1.at[band, :], group).wait()
            again = clamp(x_ref[band, :], peer1[band, :])
            x_ref[band, :] = again
            r_ref[band, :] = load_ref[band, :]
            begin(parity, group, again)

        def arrive(at):
            col_copy(parity, group, order[at], order[at], own_send.at[group, 0]).wait_recv()

        def pass_on(at):
            @pl.when(inner)
            def _():
                arrive(at)
                col_copy(parity, group, order[at], col_mate, pass_send.at[group, at - 2]).start()

        def take(at):
            if hub and at >= 2:
                @pl.when(jnp.logical_not(inner))
                def _():
                    arrive(at)
            else:
                arrive(at)

        @pl.when(live)
        def _():
            if hub:
                pass_on(2)
            multiply(parity, group, order[0], True)
            if hub:
                pass_on(3)
            for at in range(1, n_col - 1):
                take(at)
                multiply(parity, group, order[at], False)

        @pl.when(h >= 1)
        def _():
            total = partial[late, core, far] + core_in[late_parity, late, far]
            for shift in range(1, n_far):
                far_copy(late_parity, late, shift).wait()
                total = total + far_in[late_parity, late, shift - 1]
            for copy in own_copies(late_parity, late):
                copy.wait_send()
            if hub:
                @pl.when(inner)
                def _():
                    for at in range(2):
                        col_copy(late_parity, late, order[at + 2], col_mate, pass_send.at[late, at]).wait_send()
            band = pl.ds(pl.multiple_of(late * part, part), part)
            resid = r_ref[band, :] - total
            r_ref[band, :] = resid

            @pl.when(late_time != 2 * K)
            def _():
                step = late_time % K
                move = coef_ref[step] * direction[band, :] + coef_ref[K + step] * resid
                direction[band, :] = move
                answer = x_ref[band, :] + move
                x_ref[band, :] = answer

                @pl.when(late_time != K - 1)
                def _():
                    begin(1 - late_parity, late, move)

                @pl.when(late_time == K - 1)
                def _():
                    peer_copy(x_ref.at[band, :], peer1.at[band, :], late).start()

        @pl.when(live)
        def _():
            take(n_col - 1)
            multiply(parity, group, order[n_col - 1], False, 0, n_far)
            core_copy(parity, group).start()
            multiply(parity, group, order[n_col - 1], False, n_far, n_row)

        return carry

    lax.fori_loop(0, applies * GROUPS + 1, half_step, 0)


def coefficients(bounds):
    lower = bounds[0, 0].astype(jnp.float32)
    upper = bounds[0, 1].astype(jnp.float32)
    theta = 0.5 * (upper + lower)
    delta = 0.5 * (upper - lower)
    sigma = theta / delta
    rho = delta / theta
    keep, add = [jnp.zeros_like(theta)], [1.0 / theta]
    for _ in range(K - 1):
        rho_new = 1.0 / (2.0 * sigma - rho)
        keep.append(rho_new * rho)
        add.append(2.0 * rho_new / delta)
        rho = rho_new
    return jnp.stack(keep + add)


def per_device(n_row, n_col, lam_start, load, operator, partner, active, bounds):
    rows, width = lam_start.shape[1:]
    tile = operator.reshape(operator.shape[1], operator.shape[2], operator.shape[4])
    chunk = min(256, tile.shape[0])
    part = rows // GROUPS
    n_far = n_row // 2
    f32, bf16 = jnp.float32, jnp.bfloat16
    vmem = pl.BlockSpec(memory_space=pltpu.VMEM)
    dma = pltpu.SemaphoreType.DMA
    flops = 2 * (2 * K + 1) * rows * tile.size
    answer, resid = pl.pallas_call(
        functools.partial(kernel, n_row, n_col),
        out_shape=[jax.ShapeDtypeStruct((rows, width), f32)] * 2,
        in_specs=[
            pl.BlockSpec(memory_space=pltpu.SMEM), vmem, vmem, pl.BlockSpec(memory_space=pl.ANY), vmem, vmem,
        ],
        out_specs=[vmem, vmem],
        scratch_shapes=[
            pltpu.VMEM((tile.shape[0], n_row * width), bf16),
            pltpu.VMEM((2, chunk, n_row, width), bf16),
            pltpu.VMEM((2, chunk, n_row, 128), f32),
            pltpu.VMEM((2, GROUPS, n_col, part, width), bf16),
            pltpu.VMEM((GROUPS, 2, n_far, part, width), f32),
            pltpu.VMEM((2, GROUPS, n_far, part, width), f32),
            pltpu.VMEM((GROUPS, n_far - 1, part, width), f32),
            pltpu.VMEM((2, GROUPS, n_far - 1, part, width), f32),
            pltpu.VMEM((rows, width), f32),
            pltpu.VMEM((rows, width), f32),
            pltpu.VMEM((width, width), bf16),
            pltpu.VMEM((1, width), f32),
            pltpu.VMEM((rows, width), f32),
            dma((2,)),
            dma((GROUPS, n_col - 1)),
            dma((GROUPS, 2)),
            dma((2, GROUPS, n_col)),
            dma((GROUPS,)),
            dma((2, GROUPS)),
            dma((GROUPS, n_far - 1)),
            dma((2, GROUPS, n_far - 1)),
            dma((2 * GROUPS,)),
            dma((2 * GROUPS,)),
        ],
        compiler_params=pltpu.CompilerParams(
            collective_id=0, has_side_effects=True, vmem_limit_bytes=58 * 1024 * 1024
        ),
        cost_estimate=pl.CostEstimate(flops=flops, bytes_accessed=2 * tile.size, transcendentals=0),
    )(coefficients(bounds), lam_start[0], load[0], tile, partner, active[None])
    return (answer[None], resid[None])


def solution(mesh):
    return jax.shard_map(
        functools.partial(per_device, mesh.shape["row"], mesh.shape["col"]),
        mesh=mesh,
        in_specs=(
            P("body", None, ("row", "col")),
            P("body", None, ("row", "col")),
            P("body", "row", None, "col", None),
            P("body", ("row", "col")),
            P(("row", "col")),
            P("body", None),
        ),
        out_specs=(P("body", None, ("row", "col")), P("body", None, ("row", "col"))),
        check_vma=False,
    )
```
